512 devices in a mesh: grp: 8 (over x, core), dev: 64 (over z, y).
Axes of the slice: x: 4, y: 4, z: 16, core: 2. Of those that a mesh axis runs over, the one named last changes fastest.
Arguments:
- embeddings: bfloat16 [196608, 1024], P(('grp', 'dev')), may hold values from -6 to 6
- cluster_ids: int32 [196608], P(('grp', 'dev')), may hold values from 0 to 255, never falling along the last dimension, each value on 1 to 1537 neighbouring positions
Outputs:
- neighbour_mean: float32 [196608, 1024], P(('grp', 'dev'))
- log_count: float32 [196608], P(('grp', 'dev'))
The draws below stay inside these ranges and needn't reach their ends.
Inputs may be any that keep to these rules, and one draw needn't show every extreme that they name: cluster_ids never fall along the clips, so each cluster's clips are consecutive; each cluster has 1 to (5 - 1) * 384 + 1 clips and one has exactly that many; every cluster appears.
All inputs are finite; a program needn't handle non-finite values.
Results may differ from the reference program's by a relative error of at most 0.0078.
Values may be sent and summed in bfloat16 or wider, within the bound.
No kernel may reach another device: no remote copies, remote signals or barrier semaphores. Data moves between devices by JAX's collectives and lax.ppermute only.
A program may use at most 64 MiB of HBM per device.

```python
import math
import jax
import jax.numpy as jnp
import numpy as np
from jax import lax

D = 1024
CLUSTERS = 256
ROWS = 384
SPAN = 5
CLIPS = 196608


def levels(key, shape, split, low, high):
    loudness, own = 1.0, jax.random.fold_in(key, 6)
    for dim, blocks in split:
        steps = jnp.exp(jax.random.uniform(jax.random.fold_in(own, dim), (blocks,), jnp.float32, low / len(split), high / len(split)))
        loudness = loudness * jnp.repeat(steps, shape[dim] // blocks).reshape([-1 if axis == dim else 1 for axis in range(len(shape))])
    return loudness


def length_profile(amount, total, most, lean):
    weights = [(1 << 20) // math.isqrt(standing ** lean) + 1 for standing in range(2, amount + 1)]
    spare, given = total - most - (amount - 1), [1] * (amount - 1)
    while spare > 0:
        candidates = [i for i in range(amount - 1) if given[i] < most]
        whole, left = sum([weights[i] for i in candidates]), spare
        for i in candidates:
            addition = min(most - given[i], max(1, left * weights[i] // whole), spare)
            given[i] = given[i] + addition
            spare = spare - addition
    return np.array([most] + given)


def uneven(rng, amount, total, bound, slope):
    if amount == 2:
        one = jax.random.randint(rng, (), max(1, total - bound), min(bound, total - 1) + 1)
        return jnp.stack([one, total - one])
    tallies = jnp.asarray(length_profile(amount, total, bound, slope), jnp.int32)
    twos = (amount - 1) // 2
    source_of, receiver = tallies[1:1 + 2 * twos:2], tallies[2:2 + 2 * twos:2]
    slack = jnp.minimum(source_of - 1, bound - receiver)
    moved = jax.random.randint(jax.random.fold_in(rng, 1), (twos,), 0, 1 << 20) % (slack + 1)
    tallies = tallies.at[1:1 + 2 * twos:2].set(source_of - moved).at[2:2 + 2 * twos:2].set(receiver + moved)
    return tallies[jax.random.permutation(jax.random.fold_in(rng, 2), amount)]


def bell_draw(own_key, shape, width, limit, split=(), kind=jnp.bfloat16):
    values = jax.random.normal(own_key, shape, jnp.float32) * width
    if len(split) > 0:
        values = levels(own_key, shape, split, -0.22, 0.18) * values
    return jnp.clip(values, min=-limit, max=limit).astype(kind)


def setup_inputs(seed: int = 0) -> dict:
    keys = jax.random.split(jax.random.key(seed), 3)
    return {
        "embeddings": bell_draw(keys[0], (CLIPS, D), 1.0, 6.0, ((0, 512),)),
        "cluster_ids": jnp.searchsorted(jnp.cumsum(uneven(keys[1], CLUSTERS, CLIPS, (SPAN - 1) * ROWS + 1, 2)), jnp.arange(CLIPS), side="right").astype(jnp.int32),
    }


def reference(embeddings, cluster_ids):
    values = embeddings.astype(jnp.float32)
    unit_rows = (values * lax.rsqrt(lax.optimization_barrier(jnp.mean(values * values, axis=1, keepdims=True)) + 1e-06)).astype(jnp.bfloat16)
    margin = (SPAN - 1) * ROWS
    window_size = (2 * SPAN - 1) * ROWS
    padded_rows = jnp.pad(unit_rows, ((margin, margin), (0, 0)))
    padded_label = jnp.pad(cluster_ids, (margin, margin), constant_values=-1)
    kernel_scale = 2.0 / math.sqrt(D)

    def one_block(block_index):
        start = (block_index * ROWS).astype(jnp.int32)
        block_rows = lax.dynamic_slice_in_dim(unit_rows, start, ROWS, 0)
        block_label = lax.dynamic_slice_in_dim(cluster_ids, start, ROWS, 0)
        window = lax.dynamic_slice_in_dim(padded_rows, start, window_size, 0)
        window_label = lax.dynamic_slice_in_dim(padded_label, start, window_size, 0)
        scores = jnp.dot(block_rows, window.T, preferred_element_type=jnp.float32) * kernel_scale
        matched = block_label[:, None] == window_label[None, :]
        own_pair = jnp.arange(ROWS, dtype=jnp.int32)[:, None] + margin == jnp.arange(window_size, dtype=jnp.int32)[None, :]
        weight = jnp.where(matched & jnp.logical_not(own_pair), jnp.exp(scores), jnp.zeros_like(scores))
        counted = lax.optimization_barrier(jnp.sum(weight, axis=1))
        pulled = jnp.dot(weight.astype(jnp.bfloat16), window, preferred_element_type=jnp.float32)
        return (pulled / (1.0 + counted)[:, None], jnp.log(1.0 + counted))
    means, logs = lax.map(one_block, jnp.arange(CLIPS // ROWS, dtype=jnp.int32))
    return (means.reshape(CLIPS, D), logs.reshape(CLIPS))
```

```python
import math

import jax
import jax.numpy as jnp
from jax import lax
from jax.experimental import pallas as pl
from jax.experimental.pallas import tpu as pltpu
from jax.sharding import PartitionSpec as P

AXES = ("grp", "dev")
RING = 4
TAIL = 16
VMEM_BYTES = 40 * 1024 * 1024


def plane_pairs(total, up, along, columns=range(RING)):
    pairs = []
    for plane in range(total // RING):
        if 0 <= plane + up < total // RING:
            for column in columns:
                target = (column + along) % RING
                pairs.append((plane * RING + column, (plane + up) * RING + target))
    return pairs


def send(block, pairs):
    return lax.ppermute(block, AXES, pairs)


def pack_kernel(values_ref, label_ref, packed_ref):
    rows, width = values_ref.shape
    values = values_ref[...].astype(jnp.float32)
    scale = lax.rsqrt(jnp.mean(values * values, axis=1, keepdims=True) + 1e-06)
    packed_ref[:rows, :] = (values * scale).astype(jnp.bfloat16)
    label = (label_ref[...] + 1).astype(jnp.float32).astype(jnp.bfloat16)
    packed_ref[rows:, :rows] = jnp.broadcast_to(label, (TAIL, rows))
    packed_ref[rows:, rows:] = jnp.zeros((TAIL, width - rows), jnp.bfloat16)


def tile(own, own_label, far_ref, kernel_scale, diagonal):
    rows = own.shape[0]
    far = far_ref[:rows, :]
    far_label = far_ref[rows : rows + TAIL, :rows].astype(jnp.float32)[:1, :]
    scores = (
        lax.dot_general(own, far, (((1,), (1,)), ((), ())), preferred_element_type=jnp.float32)
        * kernel_scale
    )
    linked = own_label == far_label
    if diagonal:
        linked = linked & (
            lax.broadcasted_iota(jnp.int32, (rows, rows), 0)
            != lax.broadcasted_iota(jnp.int32, (rows, rows), 1)
        )
    weight = jnp.where(linked, jnp.exp(scores), 0.0)
    pull = jnp.dot(weight.astype(jnp.bfloat16), far, preferred_element_type=jnp.float32)
    return pull, jnp.sum(weight, axis=1, keepdims=True)


def first_kernel(kernel_scale, own_ref, *refs):
    far_refs, (pulled_ref, counted_ref) = refs[:-2], refs[-2:]
    rows = pulled_ref.shape[0]
    own = own_ref[:rows, :]
    label = own_ref[rows:, :rows].astype(jnp.float32)[:1, :]
    own_label = jnp.broadcast_to(label, (128, rows)).T[:, :1]
    pulled, counted = tile(own, own_label, own_ref, kernel_scale, True)
    for far_ref in far_refs:
        pull, count = tile(own, own_label, far_ref, kernel_scale, False)
        pulled, counted = pulled + pull, counted + count
    pulled_ref[...] = pulled
    counted_ref[...] = jnp.broadcast_to(counted, counted_ref.shape)


def last_kernel(kernel_scale, own_ref, pulled_ref, counted_ref, *refs):
    far_refs, (mean_ref, log_ref) = refs[:-2], refs[-2:]
    rows = pulled_ref.shape[0]
    own = own_ref[:rows, :]
    label = own_ref[rows:, :rows].astype(jnp.float32)[:1, :]
    own_label = jnp.broadcast_to(label, (128, rows)).T[:, :1]
    pulled, counted = pulled_ref[...], counted_ref[:, :1]
    for far_ref in far_refs:
        pull, count = tile(own, own_label, far_ref, kernel_scale, False)
        pulled, counted = pulled + pull, counted + count
    mean_ref[...] = pulled / (1.0 + counted)
    log_ref[...] = jnp.log(1.0 + jnp.broadcast_to(counted, (rows, 128)).T[:1, :])


def cost(tiles, rows, width):
    return pl.CostEstimate(
        flops=4 * tiles * rows * rows * width,
        bytes_accessed=2 * (tiles + 1) * rows * width,
        transcendentals=tiles * rows * rows,
    )


def shards(embeddings, cluster_ids):
    rows, width = embeddings.shape
    total = lax.axis_size("grp") * lax.axis_size("dev")
    kernel_scale = 2.0 / math.sqrt(width)
    params = pltpu.CompilerParams(vmem_limit_bytes=VMEM_BYTES)
    own = pl.pallas_call(
        pack_kernel,
        out_shape=jax.ShapeDtypeStruct((rows + TAIL, width), jnp.bfloat16),
        compiler_params=params,
        name="pack",
    )(embeddings, cluster_ids.reshape(1, rows))
    column = lax.rem(lax.axis_index("dev"), RING)

    below = send(own, plane_pairs(total, 1, 0))
    above = send(own, plane_pairs(total, -1, 0))
    across = send(own, plane_pairs(total, 0, 2))
    left = send(own, plane_pairs(total, 0, 1))
    right = send(own, plane_pairs(total, 0, -1))
    side_down = send(jnp.where(column == 0, above, below), plane_pairs(total, 0, -1))
    side_up = send(jnp.where(column == RING - 1, below, above), plane_pairs(total, 0, 1))
    corner = send(
        across,
        plane_pairs(total, 1, 0, range(RING // 2))
        + plane_pairs(total, -1, 0, range(RING // 2, RING)),
    )

    near = (below, above, left, right, across)
    pulled, counted = pl.pallas_call(
        lambda *refs: first_kernel(kernel_scale, *refs),
        out_shape=(
            jax.ShapeDtypeStruct((rows, width), jnp.float32),
            jax.ShapeDtypeStruct((rows, 128), jnp.float32),
        ),
        compiler_params=params,
        cost_estimate=cost(1 + len(near), rows, width),
        name="near",
    )(own, *near)
    late = (side_down, side_up, corner)
    neighbour_mean, log_count = pl.pallas_call(
        lambda *refs: last_kernel(kernel_scale, *refs),
        out_shape=(
            jax.ShapeDtypeStruct((rows, width), jnp.float32),
            jax.ShapeDtypeStruct((1, rows), jnp.float32),
        ),
        compiler_params=params,
        cost_estimate=cost(len(late), rows, width),
        name="late",
    )(own, pulled, counted, *late)
    return neighbour_mean, log_count.reshape(rows)


def solution(mesh):
    placed = (P(AXES, None), P(AXES))
    return jax.shard_map(
        shards,
        mesh=mesh,
        in_specs=placed,
        out_specs=placed,
        check_vma=False,
    )
```

```python
import functools
import math

import jax
import jax.numpy as jnp
from jax import lax
from jax.experimental import pallas as pl
from jax.experimental.pallas import tpu as pltpu
from jax.sharding import PartitionSpec as P

AXES = ("grp", "dev")
ROWS = 384
RING = 4
TAIL = 8
VMEM_BYTES = 40 * 1024 * 1024


def plane_pairs(total, up, along, columns=range(RING)):
    pairs = []
    for plane in range(total // RING):
        if 0 <= plane + up < total // RING:
            for column in columns:
                target = (column + along) % RING
                pairs.append((plane * RING + column, (plane + up) * RING + target))
    return pairs


def swaps(total, stride, start):
    pairs = []
    for low in range(start * stride, total - stride, 2 * stride):
        for device in range(low, low + stride):
            pairs += [(device, device + stride), (device + stride, device)]
    return pairs


def ring_swaps(total, start):
    pairs = []
    for plane in range(0, total, RING):
        for column in range(start, start + RING, 2):
            one, other = plane + column % RING, plane + (column + 1) % RING
            pairs += [(one, other), (other, one)]
    return pairs


def send(block, pairs):
    return lax.ppermute(block, AXES, pairs)


def pack_kernel(values_ref, label_ref, packed_ref):
    rows, width = values_ref.shape
    values = values_ref[...].astype(jnp.float32)
    scale = lax.rsqrt(jnp.mean(values * values, axis=1, keepdims=True) + 1e-06)
    packed_ref[:rows, :] = (values * scale).astype(jnp.bfloat16)
    label = (label_ref[...].reshape(1, rows) + 1).astype(jnp.float32).astype(jnp.bfloat16)
    packed_ref[rows:, :rows] = jnp.broadcast_to(label, (TAIL, rows))
    packed_ref[rows:, rows:] = jnp.zeros((TAIL, width - rows), jnp.bfloat16)


def labels_of(tail_ref):
    rows = tail_ref.shape[0] - TAIL
    return tail_ref[rows:, :ROWS].astype(jnp.float32)[:1, :]


def tile(own, own_label, far, far_label, kernel_scale, diagonal):
    scores = (
        lax.dot_general(own, far, (((1,), (1,)), ((), ())), preferred_element_type=jnp.float32)
        * kernel_scale
    )
    linked = own_label == far_label
    if diagonal:
        shape = scores.shape
        linked = linked & (
            lax.broadcasted_iota(jnp.int32, shape, 0) != lax.broadcasted_iota(jnp.int32, shape, 1)
        )
    weight = jnp.where(linked, jnp.exp(scores), 0.0)
    pull = jnp.dot(weight.astype(jnp.bfloat16), far, preferred_element_type=jnp.float32)
    return pull, jnp.sum(weight, axis=1, keepdims=True)


def block_kernel(kernel_scale, fresh, final, n_blocks, n_halves, own_ref, *refs):
    refs, (sum_ref, count_ref) = refs[:-2], refs[-2:]
    rows = own_ref.shape[0] - TAIL
    own = own_ref[:rows, :]
    own_row = labels_of(own_ref)
    own_label = jnp.broadcast_to(own_row, (128, rows)).T[:, :1]
    if fresh:
        pulled, counted = tile(own, own_label, own, own_row, kernel_scale, True)
    else:
        pulled, counted = refs[0][...], refs[1][:, :1]
        refs = refs[2:]
    parts = [(ref[:rows, :], labels_of(ref)) for ref in refs[:n_blocks]]
    for i in range(n_halves):
        top, bottom = refs[n_blocks + 2 * i], refs[n_blocks + 2 * i + 1]
        label, half = labels_of(bottom), top.shape[0]
        parts += [(top[...], label[:, :half]), (bottom[: rows - half, :], label[:, half:])]
    for far, far_label in parts:
        pull, count = tile(own, own_label, far, far_label, kernel_scale, False)
        pulled, counted = pulled + pull, counted + count
    if final:
        sum_ref[...] = pulled * (1.0 / (1.0 + counted))
        logs = jnp.log(1.0 + jnp.broadcast_to(counted, (rows, 128)).T[:1, :])
        count_ref[...] = logs.reshape(rows)
    else:
        sum_ref[...] = pulled
        count_ref[...] = jnp.broadcast_to(counted, count_ref.shape)


def cost(tiles, rows, width):
    return pl.CostEstimate(
        flops=4 * tiles * rows * rows * width,
        bytes_accessed=2 * (tiles + 1) * rows * width,
        transcendentals=tiles * rows * rows,
    )


def shards(embeddings, cluster_ids):
    rows, width = embeddings.shape
    total = lax.axis_size("grp") * lax.axis_size("dev")
    kernel_scale = 2.0 / math.sqrt(width)
    params = pltpu.CompilerParams(vmem_limit_bytes=VMEM_BYTES)
    block = jax.ShapeDtypeStruct((rows + TAIL, width), jnp.bfloat16)
    sums = jax.ShapeDtypeStruct((rows, width), jnp.float32)
    counts = jax.ShapeDtypeStruct((rows, 128), jnp.float32)
    own = pl.pallas_call(
        pack_kernel,
        out_shape=block,
        compiler_params=params,
        name="pack",
    )(embeddings, cluster_ids)
    column = lax.rem(lax.axis_index("dev"), RING)
    odd = lax.rem(lax.axis_index("dev") // RING, 2)

    def add(state, blocks, halves, final, name):
        return pl.pallas_call(
            functools.partial(block_kernel, kernel_scale, not state, final, len(blocks), len(halves) // 2),
            out_shape=(sums, jax.ShapeDtypeStruct((rows,), jnp.float32) if final else counts),
            compiler_params=params,
            cost_estimate=cost(len(blocks) + len(halves) // 2 + (not state), rows, width),
            name=name,
        )(own, *state, *blocks, *halves)

    across = send(own, plane_pairs(total, 0, 2))
    below = send(own, plane_pairs(total, 1, 0))
    above = send(own, plane_pairs(total, -1, 0))
    first_column = send(own, ring_swaps(total, 0))
    second_column = send(own, ring_swaps(total, 1))
    climb = plane_pairs(total, 1, 0, range(RING // 2)) + plane_pairs(
        total, -1, 0, range(RING // 2, RING)
    )
    corner = send(across, climb)
    first_side = send(jnp.where(lax.rem(column, 2) == 1, below, above), ring_swaps(total, 0))
    second_side = send(jnp.where(column >= RING // 2, below, above), ring_swaps(total, 1))
    state = add((), (across, above, below, first_column, second_column), (), False, "near")
    state = add(state, (corner,), (), False, "corner")
    state = add(state, (first_side,), (), False, "side")
    return add(state, (second_side,), (), True, "late")


def solution(mesh):
    placed = (P(AXES, None), P(AXES))
    return jax.shard_map(
        shards,
        mesh=mesh,
        in_specs=placed,
        out_specs=placed,
        check_vma=False,
    )
```

```python
import functools
import math

import jax
import jax.numpy as jnp
from jax import lax
from jax.experimental import pallas as pl
from jax.experimental.pallas import tpu as pltpu
from jax.sharding import PartitionSpec as P

AXES = ("grp", "dev")
ROWS = 384
RING = 4
CHUNKS = 2
TAIL = 8
VMEM_BYTES = 40 * 1024 * 1024


def plane_pairs(total, up, along, columns=range(RING)):
    pairs = []
    for plane in range(total // RING):
        if 0 <= plane + up < total // RING:
            for column in columns:
                target = (column + along) % RING
                pairs.append((plane * RING + column, (plane + up) * RING + target))
    return pairs


def swaps(total, stride, start):
    pairs = []
    for low in range(start * stride, total - stride, 2 * stride):
        for device in range(low, low + stride):
            pairs += [(device, device + stride), (device + stride, device)]
    return pairs


def ring_swaps(total, start):
    pairs = []
    for plane in range(0, total, RING):
        for column in range(start, start + RING, 2):
            one, other = plane + column % RING, plane + (column + 1) % RING
            pairs += [(one, other), (other, one)]
    return pairs


def send(block, pairs):
    return lax.ppermute(block, AXES, pairs)


def pack_kernel(values_hbm, label_hbm, packed_ref, values_ref, label_ref, semaphores):
    rows, width = values_ref.shape
    label_copy = pltpu.make_async_copy(label_hbm, label_ref, semaphores.at[CHUNKS])
    chunks = [pl.ds(i * (rows // CHUNKS), rows // CHUNKS) for i in range(CHUNKS)]
    copies = [
        pltpu.make_async_copy(values_hbm.at[chunk], values_ref.at[chunk], semaphores.at[i])
        for i, chunk in enumerate(chunks)
    ]
    label_copy.start()
    for copy in copies:
        copy.start()
    packed_ref[rows:, rows:] = jnp.zeros((TAIL, width - rows), jnp.bfloat16)
    label_copy.wait()
    label = (label_ref[...].reshape(1, rows) + 1).astype(jnp.float32).astype(jnp.bfloat16)
    packed_ref[rows:, :rows] = jnp.broadcast_to(label, (TAIL, rows))
    for copy, chunk in zip(copies, chunks):
        copy.wait()
        values = values_ref[chunk, :].astype(jnp.float32)
        scale = lax.rsqrt(jnp.mean(values * values, axis=1, keepdims=True) + 1e-06)
        packed_ref[chunk, :] = (values * scale).astype(jnp.bfloat16)


def labels_of(tail_ref):
    rows = tail_ref.shape[0] - TAIL
    return tail_ref[rows:, :ROWS].astype(jnp.float32)[:1, :]


def tile(own, own_label, far, far_label, kernel_scale, diagonal):
    scores = (
        lax.dot_general(own, far, (((1,), (1,)), ((), ())), preferred_element_type=jnp.float32)
        * kernel_scale
    )
    linked = own_label == far_label
    if diagonal:
        shape = scores.shape
        linked = linked & (
            lax.broadcasted_iota(jnp.int32, shape, 0) != lax.broadcasted_iota(jnp.int32, shape, 1)
        )
    weight = jnp.where(linked, jnp.exp(scores), 0.0)
    pull = jnp.dot(weight.astype(jnp.bfloat16), far, preferred_element_type=jnp.float32)
    return pull, jnp.sum(weight, axis=1, keepdims=True)


def block_kernel(kernel_scale, fresh, final, n_blocks, n_halves, own_ref, *refs):
    refs, (sum_ref, count_ref) = refs[:-2], refs[-2:]
    rows = own_ref.shape[0] - TAIL
    own = own_ref[:rows, :]
    own_row = labels_of(own_ref)
    own_label = jnp.broadcast_to(own_row, (128, rows)).T[:, :1]
    if fresh:
        pulled, counted = tile(own, own_label, own, own_row, kernel_scale, True)
    else:
        pulled, counted = refs[0][...], refs[1][:, :1]
        refs = refs[2:]
    parts = [(ref[:rows, :], labels_of(ref)) for ref in refs[:n_blocks]]
    for i in range(n_halves):
        top, bottom = refs[n_blocks + 2 * i], refs[n_blocks + 2 * i + 1]
        label, half = labels_of(bottom), top.shape[0]
        parts += [(top[...], label[:, :half]), (bottom[: rows - half, :], label[:, half:])]
    for far, far_label in parts:
        pull, count = tile(own, own_label, far, far_label, kernel_scale, False)
        pulled, counted = pulled + pull, counted + count
    if final:
        sum_ref[...] = pulled * (1.0 / (1.0 + counted))
        logs = jnp.log(1.0 + jnp.broadcast_to(counted, (rows, 128)).T[:1, :])
        count_ref[...] = logs.reshape(rows)
    else:
        sum_ref[...] = pulled
        count_ref[...] = jnp.broadcast_to(counted, count_ref.shape)


def cost(tiles, rows, width):
    return pl.CostEstimate(
        flops=4 * tiles * rows * rows * width,
        bytes_accessed=2 * (tiles + 1) * rows * width,
        transcendentals=tiles * rows * rows,
    )


def shards(embeddings, cluster_ids):
    rows, width = embeddings.shape
    total = lax.axis_size("grp") * lax.axis_size("dev")
    kernel_scale = 2.0 / math.sqrt(width)
    params = pltpu.CompilerParams(vmem_limit_bytes=VMEM_BYTES)
    block = jax.ShapeDtypeStruct((rows + TAIL, width), jnp.bfloat16)
    sums = jax.ShapeDtypeStruct((rows, width), jnp.float32)
    counts = jax.ShapeDtypeStruct((rows, 128), jnp.float32)
    own = pl.pallas_call(
        pack_kernel,
        out_shape=block,
        in_specs=[pl.BlockSpec(memory_space=pl.ANY)] * 2,
        scratch_shapes=[
            pltpu.VMEM((rows, width), jnp.bfloat16),
            pltpu.VMEM((rows,), jnp.int32),
            pltpu.SemaphoreType.DMA((CHUNKS + 1,)),
        ],
        compiler_params=params,
        name="pack",
    )(
        pltpu.with_memory_space_constraint(embeddings, pltpu.HBM),
        pltpu.with_memory_space_constraint(cluster_ids, pltpu.HBM),
    )
    column = lax.rem(lax.axis_index("dev"), RING)
    odd = lax.rem(lax.axis_index("dev") // RING, 2)

    def add(state, blocks, halves, final, name):
        return pl.pallas_call(
            functools.partial(block_kernel, kernel_scale, not state, final, len(blocks), len(halves) // 2),
            out_shape=(sums, jax.ShapeDtypeStruct((rows,), jnp.float32) if final else counts),
            compiler_params=params,
            cost_estimate=cost(len(blocks) + len(halves) // 2 + (not state), rows, width),
            name=name,
        )(own, *state, *blocks, *halves)

    across = send(own, plane_pairs(total, 0, 2))
    below = send(own, plane_pairs(total, 1, 0))
    above = send(own, plane_pairs(total, -1, 0))
    first_column = send(own, ring_swaps(total, 0))
    second_column = send(own, ring_swaps(total, 1))
    climb = plane_pairs(total, 1, 0, range(RING // 2)) + plane_pairs(
        total, -1, 0, range(RING // 2, RING)
    )
    corner = send(across, climb)
    first_side = send(jnp.where(lax.rem(column, 2) == 1, below, above), ring_swaps(total, 0))
    second_side = send(jnp.where(column >= RING // 2, below, above), ring_swaps(total, 1))
    state = add((), (across, above, below, second_column, first_column), (), False, "near")
    state = add(state, (corner,), (), False, "corner")
    state = add(state, (first_side,), (), False, "side")
    return add(state, (second_side,), (), True, "late")


def solution(mesh):
    placed = (P(AXES, None), P(AXES))
    return jax.shard_map(
        shards,
        mesh=mesh,
        in_specs=placed,
        out_specs=placed,
        check_vma=False,
    )
```

```python
import functools
import math

import jax
import jax.numpy as jnp
from jax import lax
from jax.experimental import pallas as pl
from jax.experimental.pallas import tpu as pltpu
from jax.sharding import PartitionSpec as P

AXES = ("grp", "dev")
ROWS = 384
RING = 4
CHUNKS = 2
LANES = 128
TAIL = 16
VMEM_BYTES = 40 * 1024 * 1024


def plane_pairs(total, up, along, columns=range(RING)):
    pairs = []
    for plane in range(total // RING):
        if 0 <= plane + up < total // RING:
            for column in columns:
                target = (column + along) % RING
                pairs.append((plane * RING + column, (plane + up) * RING + target))
    return pairs


def ring_swaps(total, start):
    pairs = []
    for plane in range(0, total, RING):
        for column in range(start, start + RING, 2):
            one, other = plane + column % RING, plane + (column + 1) % RING
            pairs += [(one, other), (other, one)]
    return pairs


def send(block, pairs):
    return lax.ppermute(block, AXES, pairs)


def pack_kernel(values_hbm, label_hbm, packed_ref, values_ref, label_ref, semaphores):
    rows, width = values_ref.shape
    label_copy = pltpu.make_async_copy(label_hbm, label_ref, semaphores.at[CHUNKS])
    chunks = [pl.ds(i * (rows // CHUNKS), rows // CHUNKS) for i in range(CHUNKS)]
    copies = [
        pltpu.make_async_copy(values_hbm.at[chunk], values_ref.at[chunk], semaphores.at[i])
        for i, chunk in enumerate(chunks)
    ]
    label_copy.start()
    for copy in copies:
        copy.start()
    slabs = width // LANES
    label_copy.wait()
    label = (label_ref[...].reshape(1, rows) + 1).astype(jnp.float32)
    lines = [label[:, i : i + LANES] for i in range(0, rows, LANES)]
    blank = jnp.zeros((TAIL - len(lines), LANES), jnp.float32)
    packed_ref[slabs * rows :, :] = jnp.concatenate([*lines, blank], axis=0).astype(jnp.bfloat16)
    for i, copy in enumerate(copies):
        copy.wait()
        values = values_ref[chunks[i], :].astype(jnp.float32)
        scale = lax.rsqrt(jnp.mean(values * values, axis=1, keepdims=True) + 1e-06)
        unit = (values * scale).astype(jnp.bfloat16)
        for slab in range(slabs):
            first = slab * rows + i * (rows // CHUNKS)
            packed_ref[first : first + rows // CHUNKS, :] = unit[:, slab * LANES : (slab + 1) * LANES]


def rows_of(block_ref):
    slabs = (block_ref.shape[0] - TAIL) // ROWS
    return jnp.concatenate([block_ref[i * ROWS : (i + 1) * ROWS, :] for i in range(slabs)], axis=1)


def labels_of(block_ref):
    tail = block_ref[block_ref.shape[0] - TAIL :, :].astype(jnp.float32)
    return jnp.concatenate([tail[i : i + 1] for i in range(ROWS // LANES)], axis=1)


def tile(own, own_label, far, far_label, kernel_scale, diagonal):
    scores = (
        lax.dot_general(own, far, (((1,), (1,)), ((), ())), preferred_element_type=jnp.float32)
        * kernel_scale
    )
    linked = own_label == far_label
    if diagonal:
        shape = scores.shape
        linked = linked & (
            lax.broadcasted_iota(jnp.int32, shape, 0) != lax.broadcasted_iota(jnp.int32, shape, 1)
        )
    weight = jnp.where(linked, jnp.exp(scores), 0.0)
    pull = jnp.dot(weight.astype(jnp.bfloat16), far, preferred_element_type=jnp.float32)
    return pull, jnp.sum(weight, axis=1, keepdims=True)


def block_kernel(kernel_scale, fresh, final, own_ref, *refs):
    refs, (sum_ref, count_ref) = refs[:-2], refs[-2:]
    own, own_row = rows_of(own_ref), labels_of(own_ref)
    rows = own.shape[0]
    own_label = jnp.broadcast_to(own_row, (LANES, rows)).T[:, :1]
    if fresh:
        pulled, counted = tile(own, own_label, own, own_row, kernel_scale, True)
    else:
        pulled, counted = refs[0][...], refs[1][:, :1]
        refs = refs[2:]
    for far_ref in refs:
        pull, count = tile(
            own, own_label, rows_of(far_ref), labels_of(far_ref), kernel_scale, False
        )
        pulled, counted = pulled + pull, counted + count
    if final:
        sum_ref[...] = pulled * (1.0 / (1.0 + counted))
        logs = jnp.log(1.0 + jnp.broadcast_to(counted, (rows, 128)).T[:1, :])
        count_ref[...] = logs.reshape(rows)
    else:
        sum_ref[...] = pulled
        count_ref[...] = jnp.broadcast_to(counted, count_ref.shape)


def cost(tiles, rows, width):
    return pl.CostEstimate(
        flops=4 * tiles * rows * rows * width,
        bytes_accessed=2 * (tiles + 1) * rows * width,
        transcendentals=tiles * rows * rows,
    )


def shards(embeddings, cluster_ids):
    rows, width = embeddings.shape
    total = lax.axis_size("grp") * lax.axis_size("dev")
    kernel_scale = 2.0 / math.sqrt(width)
    params = pltpu.CompilerParams(vmem_limit_bytes=VMEM_BYTES)
    block = jax.ShapeDtypeStruct((width // LANES * rows + TAIL, LANES), jnp.bfloat16)
    sums = jax.ShapeDtypeStruct((rows, width), jnp.float32)
    counts = jax.ShapeDtypeStruct((rows, 128), jnp.float32)
    own = pl.pallas_call(
        pack_kernel,
        out_shape=block,
        in_specs=[pl.BlockSpec(memory_space=pl.ANY)] * 2,
        scratch_shapes=[
            pltpu.VMEM((rows, width), jnp.bfloat16),
            pltpu.VMEM((rows,), jnp.int32),
            pltpu.SemaphoreType.DMA((CHUNKS + 1,)),
        ],
        compiler_params=params,
        name="pack",
    )(
        pltpu.with_memory_space_constraint(embeddings, pltpu.HBM),
        pltpu.with_memory_space_constraint(cluster_ids, pltpu.HBM),
    )
    column = lax.rem(lax.axis_index("dev"), RING)

    def add(state, blocks, final, name):
        return pl.pallas_call(
            functools.partial(block_kernel, kernel_scale, not state, final),
            out_shape=(sums, jax.ShapeDtypeStruct((rows,), jnp.float32) if final else counts),
            compiler_params=params,
            cost_estimate=cost(len(blocks) + (not state), rows, width),
            name=name,
        )(own, *state, *blocks)

    across = send(own, plane_pairs(total, 0, 2))
    below = send(own, plane_pairs(total, 1, 0))
    above = send(own, plane_pairs(total, -1, 0))
    first_column = send(own, ring_swaps(total, 0))
    second_column = send(own, ring_swaps(total, 1))
    climb = plane_pairs(total, 1, 0, range(RING // 2)) + plane_pairs(
        total, -1, 0, range(RING // 2, RING)
    )
    corner = send(across, climb)
    first_side = send(jnp.where(lax.rem(column, 2) == 1, below, above), ring_swaps(total, 0))
    second_side = send(jnp.where(column >= RING // 2, below, above), ring_swaps(total, 1))
    state = add((), (across, above, below, second_column, first_column), False, "near")
    state = add(state, (corner,), False, "corner")
    state = add(state, (first_side,), False, "side")
    return add(state, (second_side,), True, "late")


def solution(mesh):
    placed = (P(AXES, None), P(AXES))
    return jax.shard_map(
        shards,
        mesh=mesh,
        in_specs=placed,
        out_specs=placed,
        check_vma=False,
    )
```

```python
import functools
import math

import jax
import jax.numpy as jnp
from jax import lax
from jax.experimental import pallas as pl
from jax.experimental.pallas import tpu as pltpu
from jax.sharding import PartitionSpec as P

AXES = ("grp", "dev")
ROWS = 384
RING = 4
CHUNKS = 2
PARTS = 2
LANES = 128
TAIL = 16
VMEM_BYTES = 40 * 1024 * 1024


def plane_pairs(total, up, along, columns=range(RING)):
    pairs = []
    for plane in range(total // RING):
        if 0 <= plane + up < total // RING:
            for column in columns:
                target = (column + along) % RING
                pairs.append((plane * RING + column, (plane + up) * RING + target))
    return pairs


def ring_swaps(total, start):
    pairs = []
    for plane in range(0, total, RING):
        for column in range(start, start + RING, 2):
            one, other = plane + column % RING, plane + (column + 1) % RING
            pairs += [(one, other), (other, one)]
    return pairs


def send(block, pairs):
    return lax.ppermute(block, AXES, pairs)


def pack_kernel(values_hbm, label_hbm, packed_ref, values_ref, label_ref, semaphores):
    rows, width = values_ref.shape
    label_copy = pltpu.make_async_copy(label_hbm, label_ref, semaphores.at[CHUNKS])
    chunks = [pl.ds(i * (rows // CHUNKS), rows // CHUNKS) for i in range(CHUNKS)]
    copies = [
        pltpu.make_async_copy(values_hbm.at[chunk], values_ref.at[chunk], semaphores.at[i])
        for i, chunk in enumerate(chunks)
    ]
    label_copy.start()
    for copy in copies:
        copy.start()
    slabs = width // LANES
    label_copy.wait()
    label = (label_ref[...].reshape(1, rows) + 1).astype(jnp.float32)
    lines = [label[:, i : i + LANES] for i in range(0, rows, LANES)]
    blank = jnp.zeros((TAIL - len(lines), LANES), jnp.float32)
    packed_ref[slabs * rows :, :] = jnp.concatenate([*lines, blank], axis=0).astype(jnp.bfloat16)
    for i, copy in enumerate(copies):
        copy.wait()
        values = values_ref[chunks[i], :].astype(jnp.float32)
        scale = lax.rsqrt(jnp.mean(values * values, axis=1, keepdims=True) + 1e-06)
        unit = (values * scale).astype(jnp.bfloat16)
        for slab in range(slabs):
            first = slab * rows + i * (rows // CHUNKS)
            packed_ref[first : first + rows // CHUNKS, :] = unit[:, slab * LANES : (slab + 1) * LANES]


def rows_of(block_ref):
    slabs = (block_ref.shape[0] - TAIL) // ROWS
    return jnp.concatenate([block_ref[i * ROWS : (i + 1) * ROWS, :] for i in range(slabs)], axis=1)


def labels_of(block_ref):
    tail = block_ref[block_ref.shape[0] - TAIL :, :].astype(jnp.float32)
    return jnp.concatenate([tail[i : i + 1] for i in range(ROWS // LANES)], axis=1)


def own_column(own_row):
    return jnp.broadcast_to(own_row, (LANES, own_row.shape[1])).T[:, :1]


def weights(own, own_label, far, far_label, kernel_scale, diagonal):
    scores = (
        lax.dot_general(own, far, (((1,), (1,)), ((), ())), preferred_element_type=jnp.float32)
        * kernel_scale
    )
    linked = own_label == far_label
    if diagonal:
        shape = scores.shape
        linked = linked & (
            lax.broadcasted_iota(jnp.int32, shape, 0) != lax.broadcasted_iota(jnp.int32, shape, 1)
        )
    return jnp.where(linked, jnp.exp(scores), 0.0)


def tile(own, own_label, far, far_label, kernel_scale, diagonal):
    weight = weights(own, own_label, far, far_label, kernel_scale, diagonal)
    pull = jnp.dot(weight.astype(jnp.bfloat16), far, preferred_element_type=jnp.float32)
    return pull, jnp.sum(weight, axis=1, keepdims=True)


def block_kernel(kernel_scale, fresh, own_ref, *refs):
    refs, (sum_ref, count_ref) = refs[:-2], refs[-2:]
    own, own_row = rows_of(own_ref), labels_of(own_ref)
    own_label = own_column(own_row)
    if fresh:
        pulled, counted = tile(own, own_label, own, own_row, kernel_scale, True)
    else:
        pulled, counted = refs[0][...], refs[1][:, :1]
        refs = refs[2:]
    for far_ref in refs:
        pull, count = tile(
            own, own_label, rows_of(far_ref), labels_of(far_ref), kernel_scale, False
        )
        pulled, counted = pulled + pull, counted + count
    sum_ref[...] = pulled
    count_ref[...] = jnp.broadcast_to(counted, count_ref.shape)


def last_kernel(
    kernel_scale,
    own_ref,
    sum_ref,
    count_ref,
    far_ref,
    mean_hbm,
    log_hbm,
    mean_ref,
    log_ref,
    semaphores,
):
    own, far = rows_of(own_ref), rows_of(far_ref)
    own_label = own_column(labels_of(own_ref))
    weight = weights(own, own_label, far, labels_of(far_ref), kernel_scale, False)
    counted = count_ref[:, :1] + jnp.sum(weight, axis=1, keepdims=True)
    share = 1.0 / (1.0 + counted)
    rounded = weight.astype(jnp.bfloat16)
    rows = own.shape[0]
    step, copies = rows // PARTS, []
    for part in range(PARTS):
        first, end = part * step, (part + 1) * step
        pull = jnp.dot(rounded[first:end], far, preferred_element_type=jnp.float32)
        mean_ref[first:end, :] = (sum_ref[first:end, :] + pull) * share[first:end]
        chunk = pl.ds(first, step)
        copies.append(
            pltpu.make_async_copy(mean_ref.at[chunk], mean_hbm.at[chunk], semaphores.at[part])
        )
        copies[-1].start()
    logs = jnp.log(1.0 + jnp.broadcast_to(counted, (rows, LANES)).T[:1, :])
    log_ref[...] = logs.reshape(rows)
    copies.append(pltpu.make_async_copy(log_ref, log_hbm, semaphores.at[PARTS]))
    copies[-1].start()
    for copy in copies:
        copy.wait()


def cost(tiles, rows, width):
    return pl.CostEstimate(
        flops=4 * tiles * rows * rows * width,
        bytes_accessed=2 * (tiles + 1) * rows * width,
        transcendentals=tiles * rows * rows,
    )


def shards(embeddings, cluster_ids):
    rows, width = embeddings.shape
    total = lax.axis_size("grp") * lax.axis_size("dev")
    kernel_scale = 2.0 / math.sqrt(width)
    params = pltpu.CompilerParams(vmem_limit_bytes=VMEM_BYTES)
    block = jax.ShapeDtypeStruct((width // LANES * rows + TAIL, LANES), jnp.bfloat16)
    sums = jax.ShapeDtypeStruct((rows, width), jnp.float32)
    counts = jax.ShapeDtypeStruct((rows, 128), jnp.float32)
    own = pl.pallas_call(
        pack_kernel,
        out_shape=block,
        in_specs=[pl.BlockSpec(memory_space=pl.ANY)] * 2,
        scratch_shapes=[
            pltpu.VMEM((rows, width), jnp.bfloat16),
            pltpu.VMEM((rows,), jnp.int32),
            pltpu.SemaphoreType.DMA((CHUNKS + 1,)),
        ],
        compiler_params=params,
        name="pack",
    )(
        pltpu.with_memory_space_constraint(embeddings, pltpu.HBM),
        pltpu.with_memory_space_constraint(cluster_ids, pltpu.HBM),
    )
    column = lax.rem(lax.axis_index("dev"), RING)

    def add(state, blocks, name):
        return pl.pallas_call(
            functools.partial(block_kernel, kernel_scale, not state),
            out_shape=(sums, counts),
            compiler_params=params,
            cost_estimate=cost(len(blocks) + (not state), rows, width),
            name=name,
        )(own, *state, *blocks)

    across = send(own, plane_pairs(total, 0, 2))
    below = send(own, plane_pairs(total, 1, 0))
    above = send(own, plane_pairs(total, -1, 0))
    first_column = send(own, ring_swaps(total, 0))
    second_column = send(own, ring_swaps(total, 1))
    climb = plane_pairs(total, 1, 0, range(RING // 2)) + plane_pairs(
        total, -1, 0, range(RING // 2, RING)
    )
    corner = send(across, climb)
    first_side = send(jnp.where(lax.rem(column, 2) == 1, below, above), ring_swaps(total, 0))
    second_side = send(jnp.where(column >= RING // 2, below, above), ring_swaps(total, 1))
    state = add((), (across, above, below, second_column, first_column), "near")
    state = add(state, (corner,), "corner")
    state = add(state, (first_side,), "side")
    return pl.pallas_call(
        functools.partial(last_kernel, kernel_scale),
        out_shape=(sums, jax.ShapeDtypeStruct((rows,), jnp.float32)),
        out_specs=(pl.BlockSpec(memory_space=pl.ANY),) * 2,
        scratch_shapes=[
            pltpu.VMEM((rows, width), jnp.float32),
            pltpu.VMEM((rows,), jnp.float32),
            pltpu.SemaphoreType.DMA((PARTS + 1,)),
        ],
        compiler_params=params,
        cost_estimate=cost(1, rows, width),
        name="late",
    )(own, *state, second_side)


def solution(mesh):
    placed = (P(AXES, None), P(AXES))
    return jax.shard_map(
        shards,
        mesh=mesh,
        in_specs=placed,
        out_specs=placed,
        check_vma=False,
    )
```

```python
import functools
import math

import jax
import jax.numpy as jnp
from jax import lax
from jax.experimental import pallas as pl
from jax.experimental.pallas import tpu as pltpu
from jax.sharding import PartitionSpec as P

AXES = ("grp", "dev")
ROWS = 384
RING = 4
CHUNKS = 2
PARTS = 2
LANES = 128
TAIL = 16
VMEM_BYTES = 20 * 1024 * 1024


def plane_pairs(total, up, along, columns=range(RING)):
    pairs = []
    for plane in range(total // RING):
        if 0 <= plane + up < total // RING:
            for column in columns:
                target = (column + along) % RING
                pairs.append((plane * RING + column, (plane + up) * RING + target))
    return pairs


def ring_swaps(total, start):
    pairs = []
    for plane in range(0, total, RING):
        for column in range(start, start + RING, 2):
            one, other = plane + column % RING, plane + (column + 1) % RING
            pairs += [(one, other), (other, one)]
    return pairs


def send(block, pairs):
    return lax.ppermute(block, AXES, pairs)


def pack_kernel(values_hbm, label_hbm, packed_ref, values_ref, label_ref, semaphores):
    rows, width = values_ref.shape
    label_copy = pltpu.make_async_copy(label_hbm, label_ref, semaphores.at[CHUNKS])
    chunks = [pl.ds(i * (rows // CHUNKS), rows // CHUNKS) for i in range(CHUNKS)]
    copies = [
        pltpu.make_async_copy(values_hbm.at[chunk], values_ref.at[chunk], semaphores.at[i])
        for i, chunk in enumerate(chunks)
    ]
    label_copy.start()
    for copy in copies:
        copy.start()
    slabs = width // LANES
    label_copy.wait()
    label = (label_ref[...].reshape(1, rows) + 1).astype(jnp.float32)
    lines = [label[:, i : i + LANES] for i in range(0, rows, LANES)]
    blank = jnp.zeros((TAIL - len(lines), LANES), jnp.float32)
    packed_ref[slabs * rows :, :] = jnp.concatenate([*lines, blank], axis=0).astype(jnp.bfloat16)
    for i, copy in enumerate(copies):
        copy.wait()
        values = values_ref[chunks[i], :].astype(jnp.float32)
        scale = lax.rsqrt(jnp.mean(values * values, axis=1, keepdims=True) + 1e-06)
        unit = (values * scale).astype(jnp.bfloat16)
        for slab in range(slabs):
            first = slab * rows + i * (rows // CHUNKS)
            packed_ref[first : first + rows // CHUNKS, :] = unit[:, slab * LANES : (slab + 1) * LANES]


def rows_of(block_ref):
    slabs = (block_ref.shape[0] - TAIL) // ROWS
    return jnp.concatenate([block_ref[i * ROWS : (i + 1) * ROWS, :] for i in range(slabs)], axis=1)


def labels_of(block_ref):
    tail = block_ref[block_ref.shape[0] - TAIL :, :].astype(jnp.float32)
    return jnp.concatenate([tail[i : i + 1] for i in range(ROWS // LANES)], axis=1)


def own_column(own_row):
    return jnp.broadcast_to(own_row, (LANES, own_row.shape[1])).T[:, :1]


def weights(own, own_label, far, far_label, kernel_scale, diagonal):
    scores = (
        lax.dot_general(own, far, (((1,), (1,)), ((), ())), preferred_element_type=jnp.float32)
        * kernel_scale
    )
    linked = own_label == far_label
    if diagonal:
        shape = scores.shape
        linked = linked & (
            lax.broadcasted_iota(jnp.int32, shape, 0) != lax.broadcasted_iota(jnp.int32, shape, 1)
        )
    return jnp.where(linked, jnp.exp(scores), 0.0)


def tile(own, own_label, far, far_label, kernel_scale, diagonal):
    weight = weights(own, own_label, far, far_label, kernel_scale, diagonal)
    pull = jnp.dot(weight.astype(jnp.bfloat16), far, preferred_element_type=jnp.float32)
    return pull, jnp.sum(weight, axis=1, keepdims=True)


def block_kernel(kernel_scale, fresh, own_ref, *refs):
    refs, (sum_ref, count_ref) = refs[:-2], refs[-2:]
    own, own_row = rows_of(own_ref), labels_of(own_ref)
    own_label = own_column(own_row)
    if fresh:
        pulled, counted = tile(own, own_label, own, own_row, kernel_scale, True)
    else:
        pulled, counted = refs[0][...], refs[1][:, :1]
        refs = refs[2:]
    for far_ref in refs:
        pull, count = tile(
            own, own_label, rows_of(far_ref), labels_of(far_ref), kernel_scale, False
        )
        pulled, counted = pulled + pull, counted + count
    sum_ref[...] = pulled
    count_ref[...] = jnp.broadcast_to(counted, count_ref.shape)


def last_kernel(
    kernel_scale,
    own_ref,
    sum_ref,
    count_ref,
    far_ref,
    mean_hbm,
    log_hbm,
    mean_ref,
    log_ref,
    semaphores,
):
    own, far = rows_of(own_ref), rows_of(far_ref)
    own_label = own_column(labels_of(own_ref))
    weight = weights(own, own_label, far, labels_of(far_ref), kernel_scale, False)
    counted = count_ref[:, :1] + jnp.sum(weight, axis=1, keepdims=True)
    share = 1.0 / (1.0 + counted)
    rounded = weight.astype(jnp.bfloat16)
    rows = own.shape[0]
    step, copies = rows // PARTS, []
    for part in range(PARTS):
        first, end = part * step, (part + 1) * step
        pull = jnp.dot(rounded[first:end], far, preferred_element_type=jnp.float32)
        mean_ref[first:end, :] = (sum_ref[first:end, :] + pull) * share[first:end]
        chunk = pl.ds(first, step)
        copies.append(
            pltpu.make_async_copy(mean_ref.at[chunk], mean_hbm.at[chunk], semaphores.at[part])
        )
        copies[-1].start()
    logs = jnp.log(1.0 + jnp.broadcast_to(counted, (rows, LANES)).T[:1, :])
    log_ref[...] = logs.reshape(rows)
    copies.append(pltpu.make_async_copy(log_ref, log_hbm, semaphores.at[PARTS]))
    copies[-1].start()
    for copy in copies:
        copy.wait()


def cost(tiles, rows, width):
    return pl.CostEstimate(
        flops=4 * tiles * rows * rows * width,
        bytes_accessed=2 * (tiles + 1) * rows * width,
        transcendentals=tiles * rows * rows,
    )


def shards(embeddings, cluster_ids):
    rows, width = embeddings.shape
    total = lax.axis_size("grp") * lax.axis_size("dev")
    kernel_scale = 2.0 / math.sqrt(width)
    params = pltpu.CompilerParams(vmem_limit_bytes=VMEM_BYTES)
    block = jax.ShapeDtypeStruct((width // LANES * rows + TAIL, LANES), jnp.bfloat16)
    sums = jax.ShapeDtypeStruct((rows, width), jnp.float32)
    counts = jax.ShapeDtypeStruct((rows, 128), jnp.float32)
    own = pl.pallas_call(
        pack_kernel,
        out_shape=block,
        in_specs=[pl.BlockSpec(memory_space=pl.ANY)] * 2,
        scratch_shapes=[
            pltpu.VMEM((rows, width), jnp.bfloat16),
            pltpu.VMEM((rows,), jnp.int32),
            pltpu.SemaphoreType.DMA((CHUNKS + 1,)),
        ],
        compiler_params=params,
        name="pack",
    )(
        pltpu.with_memory_space_constraint(embeddings, pltpu.HBM),
        pltpu.with_memory_space_constraint(cluster_ids, pltpu.HBM),
    )
    column = lax.rem(lax.axis_index("dev"), RING)

    def add(state, blocks, name):
        return pl.pallas_call(
            functools.partial(block_kernel, kernel_scale, not state),
            out_shape=(sums, counts),
            compiler_params=params,
            cost_estimate=cost(len(blocks) + (not state), rows, width),
            name=name,
        )(own, *state, *blocks)

    across = send(own, plane_pairs(total, 0, 2))
    below = send(own, plane_pairs(total, 1, 0))
    above = send(own, plane_pairs(total, -1, 0))
    first_column = send(own, ring_swaps(total, 0))
    second_column = send(own, ring_swaps(total, 1))
    climb = plane_pairs(total, 1, 0, range(RING // 2)) + plane_pairs(
        total, -1, 0, range(RING // 2, RING)
    )
    corner = send(across, climb)
    first_side = send(jnp.where(lax.rem(column, 2) == 1, below, above), ring_swaps(total, 0))
    second_side = send(jnp.where(column >= RING // 2, below, above), ring_swaps(total, 1))
    state = add((), (across, above, below, second_column, first_column), "near")
    state = add(state, (corner,), "corner")
    state = add(state, (first_side,), "side")
    return pl.pallas_call(
        functools.partial(last_kernel, kernel_scale),
        out_shape=(sums, jax.ShapeDtypeStruct((rows,), jnp.float32)),
        out_specs=(pl.BlockSpec(memory_space=pl.ANY),) * 2,
        scratch_shapes=[
            pltpu.VMEM((rows, width), jnp.float32),
            pltpu.VMEM((rows,), jnp.float32),
            pltpu.SemaphoreType.DMA((PARTS + 1,)),
        ],
        compiler_params=params,
        cost_estimate=cost(1, rows, width),
        name="late",
    )(own, *state, second_side)


def solution(mesh):
    placed = (P(AXES, None), P(AXES))
    return jax.shard_map(
        shards,
        mesh=mesh,
        in_specs=placed,
        out_specs=placed,
        check_vma=False,
    )
```

```python
import functools
import math

import jax
import jax.numpy as jnp
from jax import lax
from jax.experimental import pallas as pl
from jax.experimental.pallas import tpu as pltpu
from jax.sharding import PartitionSpec as P

AXES = ("grp", "dev")
ROWS = 384
RING = 4
CHUNKS = 2
PARTS = 2
LANES = 128
TAIL = 16
VMEM_BYTES = 20 * 1024 * 1024


def plane_pairs(total, up, along, columns=range(RING)):
    pairs = []
    for plane in range(total // RING):
        if 0 <= plane + up < total // RING:
            for column in columns:
                target = (column + along) % RING
                pairs.append((plane * RING + column, (plane + up) * RING + target))
    return pairs


def ring_swaps(total, start):
    pairs = []
    for plane in range(0, total, RING):
        for column in range(start, start + RING, 2):
            one, other = plane + column % RING, plane + (column + 1) % RING
            pairs += [(one, other), (other, one)]
    return pairs


def send(block, pairs):
    return lax.ppermute(block, AXES, pairs)


def pack_kernel(values_hbm, label_hbm, packed_ref, values_ref, label_ref, semaphores):
    rows, width = values_ref.shape
    label_copy = pltpu.make_async_copy(label_hbm, label_ref, semaphores.at[CHUNKS])
    chunks = [pl.ds(i * (rows // CHUNKS), rows // CHUNKS) for i in range(CHUNKS)]
    copies = [
        pltpu.make_async_copy(values_hbm.at[chunk], values_ref.at[chunk], semaphores.at[i])
        for i, chunk in enumerate(chunks)
    ]
    label_copy.start()
    for copy in copies:
        copy.start()
    slabs = width // LANES
    label_copy.wait()
    label = (label_ref[...].reshape(1, rows) + 1).astype(jnp.float32)
    lines = [label[:, i : i + LANES] for i in range(0, rows, LANES)]
    blank = jnp.zeros((TAIL - len(lines), LANES), jnp.float32)
    packed_ref[slabs * rows :, :] = jnp.concatenate([*lines, blank], axis=0).astype(jnp.bfloat16)
    for i, copy in enumerate(copies):
        copy.wait()
        values = values_ref[chunks[i], :].astype(jnp.float32)
        scale = lax.rsqrt(jnp.mean(values * values, axis=1, keepdims=True) + 1e-06)
        unit = (values * scale).astype(jnp.bfloat16)
        for slab in range(slabs):
            first = slab * rows + i * (rows // CHUNKS)
            packed_ref[first : first + rows // CHUNKS, :] = unit[:, slab * LANES : (slab + 1) * LANES]


def rows_of(block_ref):
    slabs = (block_ref.shape[0] - TAIL) // ROWS
    return jnp.concatenate([block_ref[i * ROWS : (i + 1) * ROWS, :] for i in range(slabs)], axis=1)


def labels_of(block_ref):
    tail = block_ref[block_ref.shape[0] - TAIL :, :].astype(jnp.float32)
    return jnp.concatenate([tail[i : i + 1] for i in range(ROWS // LANES)], axis=1)


def own_column(own_row):
    return jnp.broadcast_to(own_row, (LANES, own_row.shape[1])).T[:, :1]


def weights(own, own_label, far, far_label, kernel_scale, diagonal):
    scores = (
        lax.dot_general(own, far, (((1,), (1,)), ((), ())), preferred_element_type=jnp.float32)
        * kernel_scale
    )
    linked = own_label == far_label
    if diagonal:
        shape = scores.shape
        linked = linked & (
            lax.broadcasted_iota(jnp.int32, shape, 0) != lax.broadcasted_iota(jnp.int32, shape, 1)
        )
    return jnp.where(linked, jnp.exp(scores), 0.0)


def tile(own, own_label, far, far_label, kernel_scale, diagonal):
    weight = weights(own, own_label, far, far_label, kernel_scale, diagonal)
    pull = jnp.dot(weight.astype(jnp.bfloat16), far, preferred_element_type=jnp.float32)
    return pull, jnp.sum(weight, axis=1, keepdims=True)


def block_kernel(kernel_scale, fresh, own_ref, *refs):
    refs, (sum_ref, count_ref) = refs[:-2], refs[-2:]
    own, own_row = rows_of(own_ref), labels_of(own_ref)
    own_label = own_column(own_row)
    if fresh:
        pulled, counted = tile(own, own_label, own, own_row, kernel_scale, True)
    else:
        pulled, counted = refs[0][...], refs[1][:, :1]
        refs = refs[2:]
    for far_ref in refs:
        pull, count = tile(
            own, own_label, rows_of(far_ref), labels_of(far_ref), kernel_scale, False
        )
        pulled, counted = pulled + pull, counted + count
    sum_ref[...] = pulled
    count_ref[...] = jnp.broadcast_to(counted, count_ref.shape)


def last_kernel(
    kernel_scale,
    own_ref,
    sum_ref,
    count_ref,
    far_ref,
    mean_hbm,
    log_hbm,
    mean_ref,
    log_ref,
    semaphores,
):
    own, far = rows_of(own_ref), rows_of(far_ref)
    own_label = own_column(labels_of(own_ref))
    weight = weights(own, own_label, far, labels_of(far_ref), kernel_scale, False)
    counted = count_ref[:, :1] + jnp.sum(weight, axis=1, keepdims=True)
    share = 1.0 / (1.0 + counted)
    rounded = weight.astype(jnp.bfloat16)
    rows = own.shape[0]
    step, copies = rows // PARTS, []
    for part in range(PARTS):
        first, end = part * step, (part + 1) * step
        pull = jnp.dot(rounded[first:end], far, preferred_element_type=jnp.float32)
        mean_ref[first:end, :] = (sum_ref[first:end, :] + pull) * share[first:end]
        chunk = pl.ds(first, step)
        copies.append(
            pltpu.make_async_copy(mean_ref.at[chunk], mean_hbm.at[chunk], semaphores.at[part])
        )
        copies[-1].start()
    logs = jnp.log(1.0 + jnp.broadcast_to(counted, (rows, LANES)).T[:1, :])
    log_ref[...] = logs.reshape(rows)
    copies.append(pltpu.make_async_copy(log_ref, log_hbm, semaphores.at[PARTS]))
    copies[-1].start()
    for copy in copies:
        copy.wait()


def cost(tiles, rows, width):
    return pl.CostEstimate(
        flops=4 * tiles * rows * rows * width,
        bytes_accessed=2 * (tiles + 1) * rows * width,
        transcendentals=tiles * rows * rows,
    )


def shards(embeddings, cluster_ids):
    rows, width = embeddings.shape
    total = lax.axis_size("grp") * lax.axis_size("dev")
    kernel_scale = 2.0 / math.sqrt(width)
    params = pltpu.CompilerParams(vmem_limit_bytes=VMEM_BYTES)
    block = jax.ShapeDtypeStruct((width // LANES * rows + TAIL, LANES), jnp.bfloat16)
    sums = jax.ShapeDtypeStruct((rows, width), jnp.float32)
    counts = jax.ShapeDtypeStruct((rows, 128), jnp.float32)
    own = pl.pallas_call(
        pack_kernel,
        out_shape=block,
        in_specs=[pl.BlockSpec(memory_space=pl.ANY)] * 2,
        scratch_shapes=[
            pltpu.VMEM((rows, width), jnp.bfloat16),
            pltpu.VMEM((rows,), jnp.int32),
            pltpu.SemaphoreType.DMA((CHUNKS + 1,)),
        ],
        compiler_params=params,
        name="pack",
    )(
        pltpu.with_memory_space_constraint(embeddings, pltpu.HBM),
        pltpu.with_memory_space_constraint(cluster_ids, pltpu.HBM),
    )
    column = lax.rem(lax.axis_index("dev"), RING)

    def add(state, blocks, name):
        return pl.pallas_call(
            functools.partial(block_kernel, kernel_scale, not state),
            out_shape=(sums, counts),
            compiler_params=params,
            cost_estimate=cost(len(blocks) + (not state), rows, width),
            name=name,
        )(own, *state, *blocks)

    across = send(own, plane_pairs(total, 0, 2))
    below = send(own, plane_pairs(total, 1, 0))
    above = send(own, plane_pairs(total, -1, 0))
    first_column = send(own, ring_swaps(total, 0))
    second_column = send(own, ring_swaps(total, 1))
    climb = plane_pairs(total, 1, 0, range(RING // 2)) + plane_pairs(
        total, -1, 0, range(RING // 2, RING)
    )
    corner = send(across, climb)
    first_side = send(jnp.where(lax.rem(column, 2) == 1, below, above), ring_swaps(total, 0))
    second_side = send(jnp.where(column >= RING // 2, below, above), ring_swaps(total, 1))
    state = add((), (across, below, above), "near")
    state = add(state, (first_column, second_column), "columns")
    state = add(state, (corner,), "corner")
    state = add(state, (first_side,), "side")
    return pl.pallas_call(
        functools.partial(last_kernel, kernel_scale),
        out_shape=(sums, jax.ShapeDtypeStruct((rows,), jnp.float32)),
        out_specs=(pl.BlockSpec(memory_space=pl.ANY),) * 2,
        scratch_shapes=[
            pltpu.VMEM((rows, width), jnp.float32),
            pltpu.VMEM((rows,), jnp.float32),
            pltpu.SemaphoreType.DMA((PARTS + 1,)),
        ],
        compiler_params=params,
        cost_estimate=cost(1, rows, width),
        name="late",
    )(own, *state, second_side)


def solution(mesh):
    placed = (P(AXES, None), P(AXES))
    return jax.shard_map(
        shards,
        mesh=mesh,
        in_specs=placed,
        out_specs=placed,
        check_vma=False,
    )
```

```python
import functools
import math

import jax
import jax.numpy as jnp
from jax import lax
from jax.experimental import pallas as pl
from jax.experimental.pallas import tpu as pltpu
from jax.sharding import PartitionSpec as P

AXES = ("grp", "dev")
ROWS = 384
RING = 4
CHUNKS = 2
PARTS = 2
LANES = 128
TAIL = 16
VMEM_BYTES = 20 * 1024 * 1024


def plane_pairs(total, up, along, columns=range(RING)):
    pairs = []
    for plane in range(total // RING):
        if 0 <= plane + up < total // RING:
            for column in columns:
                target = (column + along) % RING
                pairs.append((plane * RING + column, (plane + up) * RING + target))
    return pairs


def ring_swaps(total, start):
    pairs = []
    for plane in range(0, total, RING):
        for column in range(start, start + RING, 2):
            one, other = plane + column % RING, plane + (column + 1) % RING
            pairs += [(one, other), (other, one)]
    return pairs


def send(block, pairs):
    return lax.ppermute(block, AXES, pairs)


def pack_kernel(values_hbm, label_hbm, packed_ref, values_ref, label_ref, semaphores):
    rows, width = values_ref.shape
    label_copy = pltpu.make_async_copy(label_hbm, label_ref, semaphores.at[CHUNKS])
    chunks = [pl.ds(i * (rows // CHUNKS), rows // CHUNKS) for i in range(CHUNKS)]
    copies = [
        pltpu.make_async_copy(values_hbm.at[chunk], values_ref.at[chunk], semaphores.at[i])
        for i, chunk in enumerate(chunks)
    ]
    for copy in copies:
        copy.start()
    label_copy.start()
    slabs = width // LANES
    for i, copy in enumerate(copies):
        copy.wait()
        values = values_ref[chunks[i], :].astype(jnp.float32)
        scale = lax.rsqrt(jnp.mean(values * values, axis=1, keepdims=True) + 1e-06)
        unit = (values * scale).astype(jnp.bfloat16)
        for slab in range(slabs):
            first = slab * rows + i * (rows // CHUNKS)
            packed_ref[first : first + rows // CHUNKS, :] = unit[:, slab * LANES : (slab + 1) * LANES]
    label_copy.wait()
    label = (label_ref[...].reshape(1, rows) + 1).astype(jnp.float32)
    lines = [label[:, i : i + LANES] for i in range(0, rows, LANES)]
    blank = jnp.zeros((TAIL - len(lines), LANES), jnp.float32)
    packed_ref[slabs * rows :, :] = jnp.concatenate([*lines, blank], axis=0).astype(jnp.bfloat16)


def rows_of(block_ref):
    slabs = (block_ref.shape[0] - TAIL) // ROWS
    return jnp.concatenate([block_ref[i * ROWS : (i + 1) * ROWS, :] for i in range(slabs)], axis=1)


def labels_of(block_ref):
    tail = block_ref[block_ref.shape[0] - TAIL :, :].astype(jnp.float32)
    return jnp.concatenate([tail[i : i + 1] for i in range(ROWS // LANES)], axis=1)


def own_column(own_row):
    return jnp.broadcast_to(own_row, (LANES, own_row.shape[1])).T[:, :1]


def weights(own, own_label, far, far_label, kernel_scale, diagonal):
    scores = (
        lax.dot_general(own, far, (((1,), (1,)), ((), ())), preferred_element_type=jnp.float32)
        * kernel_scale
    )
    linked = own_label == far_label
    if diagonal:
        shape = scores.shape
        linked = linked & (
            lax.broadcasted_iota(jnp.int32, shape, 0) != lax.broadcasted_iota(jnp.int32, shape, 1)
        )
    return jnp.where(linked, jnp.exp(scores), 0.0)


def tile(own, own_label, far, far_label, kernel_scale, diagonal):
    weight = weights(own, own_label, far, far_label, kernel_scale, diagonal)
    pull = jnp.dot(weight.astype(jnp.bfloat16), far, preferred_element_type=jnp.float32)
    return pull, jnp.sum(weight, axis=1, keepdims=True)


def block_kernel(kernel_scale, fresh, own_ref, *refs):
    refs, (sum_ref, count_ref) = refs[:-2], refs[-2:]
    own, own_row = rows_of(own_ref), labels_of(own_ref)
    own_label = own_column(own_row)
    if fresh:
        pulled, counted = tile(own, own_label, own, own_row, kernel_scale, True)
    else:
        pulled, counted = refs[0][...], refs[1][:, :1]
        refs = refs[2:]
    for far_ref in refs:
        pull, count = tile(
            own, own_label, rows_of(far_ref), labels_of(far_ref), kernel_scale, False
        )
        pulled, counted = pulled + pull, counted + count
    sum_ref[...] = pulled
    count_ref[...] = jnp.broadcast_to(counted, count_ref.shape)


def last_kernel(
    kernel_scale,
    own_ref,
    sum_ref,
    count_ref,
    far_ref,
    mean_hbm,
    log_hbm,
    mean_ref,
    log_ref,
    semaphores,
):
    own, far = rows_of(own_ref), rows_of(far_ref)
    own_label = own_column(labels_of(own_ref))
    weight = weights(own, own_label, far, labels_of(far_ref), kernel_scale, False)
    counted = count_ref[:, :1] + jnp.sum(weight, axis=1, keepdims=True)
    share = 1.0 / (1.0 + counted)
    rounded = weight.astype(jnp.bfloat16)
    rows = own.shape[0]
    step, copies = rows // PARTS, []
    for part in range(PARTS):
        first, end = part * step, (part + 1) * step
        pull = jnp.dot(rounded[first:end], far, preferred_element_type=jnp.float32)
        mean_ref[first:end, :] = (sum_ref[first:end, :] + pull) * share[first:end]
        chunk = pl.ds(first, step)
        copies.append(
            pltpu.make_async_copy(mean_ref.at[chunk], mean_hbm.at[chunk], semaphores.at[part])
        )
        copies[-1].start()
    logs = jnp.log(1.0 + jnp.broadcast_to(counted, (rows, LANES)).T[:1, :])
    log_ref[...] = logs.reshape(rows)
    copies.append(pltpu.make_async_copy(log_ref, log_hbm, semaphores.at[PARTS]))
    copies[-1].start()
    for copy in copies:
        copy.wait()


def cost(tiles, rows, width):
    return pl.CostEstimate(
        flops=4 * tiles * rows * rows * width,
        bytes_accessed=2 * (tiles + 1) * rows * width,
        transcendentals=tiles * rows * rows,
    )


def shards(embeddings, cluster_ids):
    rows, width = embeddings.shape
    total = lax.axis_size("grp") * lax.axis_size("dev")
    kernel_scale = 2.0 / math.sqrt(width)
    params = pltpu.CompilerParams(vmem_limit_bytes=VMEM_BYTES)
    block = jax.ShapeDtypeStruct((width // LANES * rows + TAIL, LANES), jnp.bfloat16)
    sums = jax.ShapeDtypeStruct((rows, width), jnp.float32)
    counts = jax.ShapeDtypeStruct((rows, 128), jnp.float32)
    own = pl.pallas_call(
        pack_kernel,
        out_shape=block,
        in_specs=[pl.BlockSpec(memory_space=pl.ANY)] * 2,
        scratch_shapes=[
            pltpu.VMEM((rows, width), jnp.bfloat16),
            pltpu.VMEM((rows,), jnp.int32),
            pltpu.SemaphoreType.DMA((CHUNKS + 1,)),
        ],
        compiler_params=params,
        name="pack",
    )(
        pltpu.with_memory_space_constraint(embeddings, pltpu.HBM),
        pltpu.with_memory_space_constraint(cluster_ids, pltpu.HBM),
    )
    column = lax.rem(lax.axis_index("dev"), RING)

    def add(state, blocks, name):
        return pl.pallas_call(
            functools.partial(block_kernel, kernel_scale, not state),
            out_shape=(sums, counts),
            compiler_params=params,
            cost_estimate=cost(len(blocks) + (not state), rows, width),
            name=name,
        )(own, *state, *blocks)

    across = send(own, plane_pairs(total, 0, 2))
    below = send(own, plane_pairs(total, 1, 0))
    above = send(own, plane_pairs(total, -1, 0))
    first_column = send(own, ring_swaps(total, 0))
    second_column = send(own, ring_swaps(total, 1))
    climb = plane_pairs(total, 1, 0, range(RING // 2)) + plane_pairs(
        total, -1, 0, range(RING // 2, RING)
    )
    corner = send(across, climb)
    first_side = send(jnp.where(lax.rem(column, 2) == 1, below, above), ring_swaps(total, 0))
    second_side = send(jnp.where(column >= RING // 2, below, above), ring_swaps(total, 1))
    state = add((), (across, above, below, second_column, first_column), "near")
    state = add(state, (corner,), "corner")
    state = add(state, (first_side,), "side")
    return pl.pallas_call(
        functools.partial(last_kernel, kernel_scale),
        out_shape=(sums, jax.ShapeDtypeStruct((rows,), jnp.float32)),
        out_specs=(pl.BlockSpec(memory_space=pl.ANY),) * 2,
        scratch_shapes=[
            pltpu.VMEM((rows, width), jnp.float32),
            pltpu.VMEM((rows,), jnp.float32),
            pltpu.SemaphoreType.DMA((PARTS + 1,)),
        ],
        compiler_params=params,
        cost_estimate=cost(1, rows, width),
        name="late",
    )(own, *state, second_side)


def solution(mesh):
    placed = (P(AXES, None), P(AXES))
    return jax.shard_map(
        shards,
        mesh=mesh,
        in_specs=placed,
        out_specs=placed,
        check_vma=False,
    )
```
